32 devices in a mesh: rep: 2 (over x), ad: 16 (over z, y, core).
Axes of the slice: x: 2, y: 2, z: 4, core: 2. Of those that a mesh axis runs over, the one named last changes fastest.
Arguments:
- tokens: bfloat16 [16384, 8192], P(('rep', 'ad')), parts along dimension 0, may hold values from -6 to 6
- value_weight: bfloat16 [8192, 1024], P('ad'), may hold values from -0.0625 to 0.0625
- down_weight: bfloat16 [64, 8192, 64], P('ad'), may hold values from -0.0625 to 0.0625
- up_weight: bfloat16 [64, 64, 1024], P('ad'), may hold values from -0.75 to 0.75
- request_adapter: int32 [16384], P(('rep', 'ad')), parts along dimension 0, may hold values from 0 to 63, as said below
- adapter_home_slot: int32 [128], P('rep'), parts along dimension 0, may hold values from 0 to 63, as said below
Outputs:
- adapted: bfloat16 [16384, 1024], P(('rep', 'ad')), parts along dimension 0
The draws below stay inside these ranges and needn't reach their ends.
There are 2 independent parts, one for each index of `rep`. The reference program is written for one: setup_inputs(seed, part) draws one part's arguments, and reference() takes and returns one part's arrays. A program takes and returns all parts, laid end to end along the dimension named above; an argument that names none is the same for every part. Nothing has to cross between parts.
Inputs may be any that keep to these rules, and one draw needn't show every extreme that they name: `request_adapter`: among the rows of one device at most 8 name one adapter, and at most 32 name adapters whose slots have the same owner (slot // 4); every device reaches both bounds in every draw. A permutation: adapter a's panels are down_weight[adapter_home_slot[a]] and up_weight[adapter_home_slot[a]].
All inputs are finite; a program needn't handle non-finite values.
Results may differ from the reference program's by a relative error of at most 0.0037.
Values may be sent and summed in bfloat16 or wider, within the bound.
A program may use at most 192 MiB of HBM per device.

```python
import jax
import jax.numpy as jnp
from jax import lax

MODEL_DIM = 8192
VALUE_WIDTH = 1024
ADAPTER_RANK = 64
AD_DEV = 4
MOSTA = 8
TOK_DEV = 512
OWN_MOST = 32
ADAPTER_COUNT = 64
TOKENS = 8192
N_AD = 16


def routing(key):
    mapping = jax.random.permutation(jax.random.fold_in(key, 11), ADAPTER_COUNT).astype(jnp.int32)
    inverse = jnp.argsort(mapping, stable=True).astype(jnp.int32)
    spaces = N_AD * OWN_MOST
    block_keys = jax.random.split(jax.random.fold_in(key, 12), N_AD)
    scores = jax.vmap(lambda inner: jax.random.permutation(inner, spaces))(block_keys).astype(jnp.int32)
    forced = jax.random.randint(jax.random.fold_in(key, 13), (N_AD,), 0, N_AD).astype(jnp.int32)
    space_ids = jnp.arange(spaces, dtype=jnp.int32)
    in_forced = space_ids[None, :] // OWN_MOST == forced[:, None]
    scores = jnp.where(in_forced, -1 - space_ids[None, :], scores)
    chosen = jnp.argsort(scores, axis=1, stable=True)[:, :TOK_DEV].astype(jnp.int32)
    owner_of = chosen // OWN_MOST
    within = chosen % OWN_MOST
    rotate = jax.random.randint(jax.random.fold_in(key, 14), (N_AD, N_AD), 0, AD_DEV).astype(jnp.int32)
    first_local = jnp.take_along_axis(rotate, owner_of, axis=1)
    local_of = jnp.where(within < MOSTA, first_local, (first_local + 1 + (within - MOSTA) % (AD_DEV - 1)) % AD_DEV)
    adapter = inverse[owner_of * AD_DEV + local_of]
    shuffle_keys = jax.random.split(jax.random.fold_in(key, 15), N_AD)
    shuffle = jax.vmap(lambda inner: jax.random.permutation(inner, TOK_DEV))(shuffle_keys).astype(jnp.int32)
    adapter = jnp.take_along_axis(adapter, shuffle, axis=1)
    return (adapter.reshape(TOKENS).astype(jnp.int32), mapping)


def draw_request_adapter(key, part):
    return routing(key)[0]


def draw_adapter_home_slot(key, part):
    return routing(key)[1]


def steps_of(own_key, shape, shards, low, top_value):
    def one(axis_at, parts):
        heights = jax.random.uniform(jax.random.fold_in(jax.random.fold_in(own_key, 6), axis_at), (parts,), jnp.float32, low / len(shards), top_value / len(shards))
        return jnp.repeat(jnp.exp(heights), shape[axis_at] // parts).reshape((-1,) + (1,) * (len(shape) - axis_at - 1))

    gain = one(*shards[0])
    for cut in shards[1:]:
        gain = gain * one(*cut)
    return gain


def gaussian(key, extent, spread, most, cuts=(), held_as=jnp.bfloat16):
    values = spread * jax.random.normal(key, extent, jnp.float32)
    if cuts:
        values = values * steps_of(key, extent, cuts, -0.22, 0.18)
    return jnp.clip(values, -most, most).astype(held_as)


def setup_inputs(seed: int = 0, part: int = 0) -> dict:
    key_list = jax.random.split(jax.random.key(seed), 7)
    part_splits = jax.random.split(jax.random.fold_in(key_list[6], part), 7)
    tokens = gaussian(part_splits[0], (TOKENS, MODEL_DIM), 1.0, 6.0, ((0, 16),))
    value_weight = gaussian(key_list[1], (MODEL_DIM, VALUE_WIDTH), MODEL_DIM ** -0.5, 0.0625, ((0, 16),))
    down_weight = gaussian(key_list[2], (ADAPTER_COUNT, MODEL_DIM, ADAPTER_RANK), MODEL_DIM ** -0.5, 0.0625, ((0, 16),))
    up_weight = gaussian(key_list[3], (ADAPTER_COUNT, ADAPTER_RANK, VALUE_WIDTH), ADAPTER_RANK ** -0.5, 0.75, ((0, 16),))
    request_adapter = draw_request_adapter(jax.random.fold_in(jax.random.fold_in(key_list[6], part), 71), part)
    adapter_home_slot = draw_adapter_home_slot(jax.random.fold_in(jax.random.fold_in(key_list[6], part), 71), part)
    return dict(tokens=tokens, value_weight=value_weight, down_weight=down_weight, up_weight=up_weight, request_adapter=request_adapter, adapter_home_slot=adapter_home_slot)


def reference(tokens, value_weight, down_weight, up_weight, request_adapter, adapter_home_slot):
    base_output = jnp.dot(tokens, value_weight, preferred_element_type=jnp.float32)
    slot_index = adapter_home_slot[request_adapter].astype(jnp.int32)

    def single_block(blocked):
        row_block, block_slot_list = blocked
        down_matrices = down_weight[block_slot_list].astype(jnp.float32)
        rank_hidden = jnp.einsum("td,tdr->tr", row_block.astype(jnp.float32), down_matrices).astype(jnp.bfloat16)
        up_matrices = up_weight[block_slot_list].astype(jnp.float32)
        product = jnp.einsum("tr,trk->tk", rank_hidden.astype(jnp.float32), up_matrices)
        return (0.5 * product).astype(jnp.bfloat16)

    adapter_update = lax.map(single_block, (tokens.reshape(-1, 32, tokens.shape[1]), slot_index.reshape(-1, 32)))
    adapter_update = adapter_update.reshape(tokens.shape[0], value_weight.shape[1])
    return (base_output + adapter_update.astype(jnp.float32)).astype(jnp.bfloat16)
```

```python
import jax
import jax.numpy as jnp
from jax import lax
from jax.sharding import PartitionSpec as P

MOSTA = 8
PLANE = 8


def solution(mesh):
    reps, devices = mesh.shape["rep"], mesh.shape["ad"]
    inner = PLANE // reps
    layers = devices // inner
    columns = [[z * inner + j for z in range(layers)] for j in range(inner)]
    planes = [
        [r * devices + z * inner + j for r in range(reps) for j in range(inner)]
        for z in range(layers)
    ]

    def on_device(tokens, value_weight, down_weight, up_weight, request_adapter, adapter_home_slot):
        rows, model_width = tokens.shape
        resident = down_weight.shape[0]
        share = resident // reps
        adapters = adapter_home_slot.shape[0]
        rep = lax.axis_index("rep")
        labels = jnp.arange(adapters, dtype=jnp.int32)
        slot_of = jnp.sum(
            jnp.where(request_adapter[:, None] == labels[None, :], adapter_home_slot[None, :], 0),
            axis=1,
        )
        index = jnp.arange(rows, dtype=jnp.int32)
        earlier = (slot_of[:, None] == slot_of[None, :]) & (index[None, :] < index[:, None])
        position = jnp.sum(earlier.astype(jnp.int32), axis=1)
        owner, local = slot_of // resident, slot_of % resident
        layer, lane = owner // inner, owner % inner
        dest = (local // share) * inner + lane
        held = layer * share + local % share
        target = (dest * (layers * share) + held) * MOSTA + position
        places = jnp.arange(adapters * MOSTA, dtype=jnp.int32)
        pick = (places[:, None] == target[None, :]).astype(jnp.bfloat16)
        outgoing = jnp.dot(pick, tokens, preferred_element_type=jnp.float32).astype(jnp.bfloat16)
        outgoing = outgoing.reshape(PLANE, layers * share, MOSTA, model_width)
        incoming = lax.all_to_all(
            outgoing, ("rep", "ad"), split_axis=0, concat_axis=0, tiled=True, axis_index_groups=planes
        )
        down = lax.all_gather(
            lax.dynamic_slice_in_dim(down_weight, rep * share, share, 0),
            "ad", axis=0, tiled=True, axis_index_groups=columns,
        )
        up = lax.all_gather(
            lax.dynamic_slice_in_dim(up_weight, rep * share, share, 0),
            "ad", axis=0, tiled=True, axis_index_groups=columns,
        )
        whole_value = lax.all_gather(value_weight, "ad", axis=0, tiled=True)
        latent = jnp.einsum(
            "sajd,adr->sajr", incoming, down, preferred_element_type=jnp.float32
        ).astype(jnp.bfloat16)
        update = (
            0.5 * jnp.einsum("sajr,arn->sajn", latent, up, preferred_element_type=jnp.float32)
        ).astype(jnp.bfloat16)
        back = lax.all_to_all(
            update, ("rep", "ad"), split_axis=0, concat_axis=0, tiled=True, axis_index_groups=planes
        ).reshape(adapters * MOSTA, -1)
        base = jnp.dot(tokens, whole_value, preferred_element_type=jnp.float32)
        place = (target[:, None] == places[None, :]).astype(jnp.bfloat16)
        delta = jnp.dot(place, back, preferred_element_type=jnp.float32)
        return (base + delta).astype(jnp.bfloat16)

    in_specs = (
        P(("rep", "ad"), None),
        P("ad", None),
        P("ad", None, None),
        P("ad", None, None),
        P(("rep", "ad")),
        P("rep"),
    )
    return jax.shard_map(
        on_device, mesh=mesh, in_specs=in_specs, out_specs=P(("rep", "ad"), None), check_vma=False
    )
```

```python
import jax
import jax.numpy as jnp
from jax import lax
from jax.sharding import PartitionSpec as P

MOSTA = 8
PLANE = 8
F32 = jnp.float32
BF16 = jnp.bfloat16


def solution(mesh):
    reps, devices = mesh.shape["rep"], mesh.shape["ad"]
    inner = PLANE // reps
    layers = devices // inner
    relayed = layers == 4
    columns = [[z * inner + j for z in range(layers)] for j in range(inner)]
    planes = [
        [r * devices + z * inner + j for r in range(reps) for j in range(inner)]
        for z in range(layers)
    ]
    same_core = [list(range(c, devices, 2)) for c in range(2)]
    core_swap = [(i, i ^ 1) for i in range(devices)]

    def hop(array, *pairs):
        moves = [(a * inner + j, b * inner + j) for a, b in pairs for j in range(inner)]
        return lax.ppermute(array, "ad", moves)

    def exchange(array):
        return lax.all_to_all(
            array, ("rep", "ad"), split_axis=0, concat_axis=0, tiled=True, axis_index_groups=planes
        )

    def adapt(rows, panel, model_width):
        latent = jnp.einsum(
            "sajd,ard->sajr", rows, panel[:, :, :model_width], preferred_element_type=F32
        ).astype(BF16)
        return (
            0.5 * jnp.einsum("sajr,arn->sajn", latent, panel[:, :, model_width:], preferred_element_type=F32)
        ).astype(BF16)

    def after(array, earlier):
        return lax.optimization_barrier((array, earlier))[0]

    def whole_value(value_weight, earlier):
        mine = lax.all_gather(value_weight, "ad", axis=0, tiled=False, axis_index_groups=same_core)
        mine = after(mine, earlier)
        other = lax.ppermute(mine, "ad", core_swap)
        first = lax.axis_index("ad") % 2 == 0
        both = jnp.stack([jnp.where(first, mine, other), jnp.where(first, other, mine)], axis=1)
        return both.reshape(-1, value_weight.shape[1])

    def on_device(tokens, value_weight, down_weight, up_weight, request_adapter, adapter_home_slot):
        rows, model_width = tokens.shape
        resident = down_weight.shape[0]
        share = resident // reps
        adapters = adapter_home_slot.shape[0]
        rep = lax.axis_index("rep")
        here = lax.axis_index("ad") // inner
        own = jnp.concatenate(
            [
                lax.dynamic_slice_in_dim(down_weight, rep * share, share, 0).transpose(0, 2, 1),
                lax.dynamic_slice_in_dim(up_weight, rep * share, share, 0),
            ],
            axis=2,
        )
        labels = jnp.arange(adapters, dtype=jnp.int32)
        slot_of = jnp.sum(
            jnp.where(request_adapter[:, None] == labels[None, :], adapter_home_slot[None, :], 0),
            axis=1,
        )
        index = jnp.arange(rows, dtype=jnp.int32)
        earlier = (slot_of[:, None] == slot_of[None, :]) & (index[None, :] < index[:, None])
        position = jnp.sum(earlier.astype(jnp.int32), axis=1)
        owner, local = slot_of // resident, slot_of % resident
        layer, lane = owner // inner, owner % inner
        dest = (local // share) * inner + lane
        if relayed:
            low = here < 2
            middle = jnp.where(low, 2, 1)
            block = jnp.where(
                layer == here, 0, jnp.where(layer == here ^ 1, 1, jnp.where(layer == middle, 2, 3))
            )
        else:
            block = layer
        within = (local % share) * MOSTA + position
        span = share * MOSTA

        def places(start, count):
            at = jnp.arange(PLANE * count * span, dtype=jnp.int32)
            far = at // span
            return (far // count) * layers * span + (start + far % count) * span + at % span

        target = (dest * layers + block) * span + within

        def outgoing(start, count):
            pick = (places(start, count)[:, None] == target[None, :]).astype(BF16)
            sent = jnp.dot(pick, tokens, preferred_element_type=F32).astype(BF16)
            return sent.reshape(PLANE, count * share, MOSTA, model_width)

        def delta(update, start, count):
            pick = (target[:, None] == places(start, count)[None, :]).astype(BF16)
            return jnp.dot(pick, update.reshape(PLANE * count * span, -1), preferred_element_type=F32)

        def joined(parts):
            return jnp.concatenate(parts, axis=1)

        if relayed:
            edge = (here == 0) | (here == 3)
            far_rows = exchange(outgoing(3, 1))
            near_sent = outgoing(0, 3)
            near_rows = exchange(near_sent)
            pair = after(hop(own, (0, 1), (1, 0), (2, 3), (3, 2)), near_sent)
            mid = after(hop(own, (1, 2), (2, 1)), near_sent)
            crossed = hop(pair, (1, 2), (2, 1))
            outer = hop(mid, (1, 0), (2, 3))
            extra_rows = hop(far_rows, (0, 1), (3, 2))
            base = jnp.dot(tokens, whole_value(value_weight, near_sent), preferred_element_type=F32)
            extra = hop(adapt(extra_rows, crossed, model_width), (1, 0), (2, 3))
            far = jnp.where(edge, extra, adapt(far_rows, crossed, model_width))
            panels = jnp.concatenate([own, pair, jnp.where(edge, outer, mid)], axis=0)
            near = adapt(near_rows, panels, model_width)
            back = exchange(joined([near, far]))
        else:
            sent = outgoing(0, layers)
            incoming = exchange(sent)
            panels = lax.all_gather(own, "ad", axis=0, tiled=True, axis_index_groups=columns)
            base = jnp.dot(tokens, whole_value(value_weight, sent), preferred_element_type=F32)
            back = exchange(adapt(incoming, panels, model_width))
        return (base + delta(back, 0, layers)).astype(BF16)

    in_specs = (
        P(("rep", "ad"), None),
        P("ad", None),
        P("ad", None, None),
        P("ad", None, None),
        P(("rep", "ad")),
        P("rep"),
    )
    return jax.shard_map(
        on_device, mesh=mesh, in_specs=in_specs, out_specs=P(("rep", "ad"), None), check_vma=False
    )
```

```python
import jax
import jax.numpy as jnp
from jax import lax
from jax.sharding import PartitionSpec as P

MOSTA = 8
PLANE = 8
F32 = jnp.float32
BF16 = jnp.bfloat16


def solution(mesh):
    reps, devices = mesh.shape["rep"], mesh.shape["ad"]
    inner = PLANE // reps
    layers = devices // inner
    relayed = layers == 4
    columns = [[z * inner + j for z in range(layers)] for j in range(inner)]
    planes = [
        [r * devices + z * inner + j for r in range(reps) for j in range(inner)]
        for z in range(layers)
    ]

    def hop(array, *pairs):
        moves = [(a * inner + j, b * inner + j) for a, b in pairs for j in range(inner)]
        return lax.ppermute(array, "ad", moves)

    def exchange(array):
        return lax.all_to_all(
            array, ("rep", "ad"), split_axis=0, concat_axis=0, tiled=True, axis_index_groups=planes
        )

    def adapt(rows, panel, model_width):
        latent = jnp.einsum(
            "sajd,ard->sajr", rows, panel[:, :, :model_width], preferred_element_type=F32
        ).astype(BF16)
        return (
            0.5 * jnp.einsum("sajr,arn->sajn", latent, panel[:, :, model_width:], preferred_element_type=F32)
        ).astype(BF16)

    def after(array, earlier):
        return lax.optimization_barrier((array, earlier))[0]

    def swapped(array, bit):
        return lax.ppermute(array, "ad", [(i, i ^ bit) for i in range(devices)])

    def based(tokens, value_weight, earlier):
        depth = value_weight.shape[0]
        held = lax.all_gather(value_weight, "ad", axis=0, tiled=True, axis_index_groups=columns)
        held = after(held, earlier)
        pieces = {0: held}
        for bit in [1 << k for k in reversed(range(inner.bit_length() - 1))]:
            pieces.update({at ^ bit: swapped(piece, bit) for at, piece in list(pieces.items())})
        lane = lax.axis_index("ad") % inner
        columned = tokens.reshape(tokens.shape[0], layers, inner, depth)
        total = 0
        for at in sorted(pieces, key=lambda at: (at > 1, at)):
            part = lax.dynamic_slice_in_dim(columned, lane ^ at, 1, 2)
            part = part.reshape(tokens.shape[0], layers * depth)
            total = total + jnp.dot(part, pieces[at], preferred_element_type=F32)
        return total

    def on_device(tokens, value_weight, down_weight, up_weight, request_adapter, adapter_home_slot):
        rows, model_width = tokens.shape
        resident = down_weight.shape[0]
        share = resident // reps
        adapters = adapter_home_slot.shape[0]
        rep = lax.axis_index("rep")
        here = lax.axis_index("ad") // inner
        own = jnp.concatenate(
            [
                lax.dynamic_slice_in_dim(down_weight, rep * share, share, 0).transpose(0, 2, 1),
                lax.dynamic_slice_in_dim(up_weight, rep * share, share, 0),
            ],
            axis=2,
        )
        labels = jnp.arange(adapters, dtype=jnp.int32)
        slot_of = jnp.sum(
            jnp.where(request_adapter[:, None] == labels[None, :], adapter_home_slot[None, :], 0),
            axis=1,
        )
        index = jnp.arange(rows, dtype=jnp.int32)
        earlier = (slot_of[:, None] == slot_of[None, :]) & (index[None, :] < index[:, None])
        position = jnp.sum(earlier.astype(jnp.int32), axis=1)
        owner, local = slot_of // resident, slot_of % resident
        layer, lane = owner // inner, owner % inner
        dest = (local // share) * inner + lane
        if relayed:
            low = here < 2
            middle = jnp.where(low, 2, 1)
            block = jnp.where(
                layer == here, 0, jnp.where(layer == here ^ 1, 1, jnp.where(layer == middle, 2, 3))
            )
        else:
            block = layer
        within = (local % share) * MOSTA + position
        span = share * MOSTA

        def places(start, count):
            at = jnp.arange(PLANE * count * span, dtype=jnp.int32)
            far = at // span
            return (far // count) * layers * span + (start + far % count) * span + at % span

        target = (dest * layers + block) * span + within

        def outgoing(start, count):
            pick = (places(start, count)[:, None] == target[None, :]).astype(BF16)
            sent = jnp.dot(pick, tokens, preferred_element_type=F32).astype(BF16)
            return sent.reshape(PLANE, count * share, MOSTA, model_width)

        def delta(update, start, count):
            pick = (target[:, None] == places(start, count)[None, :]).astype(BF16)
            return jnp.dot(pick, update.reshape(PLANE * count * span, -1), preferred_element_type=F32)

        def joined(parts):
            return jnp.concatenate(parts, axis=1)

        if relayed:
            edge = (here == 0) | (here == 3)
            far_rows = exchange(outgoing(3, 1))
            near_sent = outgoing(0, 3)
            near_rows = exchange(near_sent)
            pair = after(hop(own, (0, 1), (1, 0), (2, 3), (3, 2)), near_sent)
            mid = after(hop(own, (1, 2), (2, 1)), near_sent)
            crossed = hop(pair, (1, 2), (2, 1))
            outer = hop(mid, (1, 0), (2, 3))
            extra_rows = hop(far_rows, (0, 1), (3, 2))
            base = based(tokens, value_weight, far_rows)
            extra = hop(adapt(extra_rows, crossed, model_width), (1, 0), (2, 3))
            far = jnp.where(edge, extra, adapt(far_rows, crossed, model_width))
            panels = jnp.concatenate([own, pair, jnp.where(edge, outer, mid)], axis=0)
            near = adapt(near_rows, panels, model_width)
            back = exchange(joined([near, far]))
        else:
            sent = outgoing(0, layers)
            incoming = exchange(sent)
            panels = lax.all_gather(own, "ad", axis=0, tiled=True, axis_index_groups=columns)
            base = based(tokens, value_weight, sent)
            back = exchange(adapt(incoming, panels, model_width))
        return (base + delta(back, 0, layers)).astype(BF16)

    in_specs = (
        P(("rep", "ad"), None),
        P("ad", None),
        P("ad", None, None),
        P("ad", None, None),
        P(("rep", "ad")),
        P("rep"),
    )
    return jax.shard_map(
        on_device, mesh=mesh, in_specs=in_specs, out_specs=P(("rep", "ad"), None), check_vma=False
    )
```

```python
import jax
import jax.numpy as jnp
from jax import lax
from jax.sharding import PartitionSpec as P

MOSTA = 8
PLANE = 8
F32 = jnp.float32
BF16 = jnp.bfloat16


def solution(mesh):
    reps, devices = mesh.shape["rep"], mesh.shape["ad"]
    inner = PLANE // reps
    layers = devices // inner
    relayed = layers == 4
    columns = [[z * inner + j for z in range(layers)] for j in range(inner)]
    planes = [
        [r * devices + z * inner + j for r in range(reps) for j in range(inner)]
        for z in range(layers)
    ]

    def hop(array, *pairs):
        moves = [(a * inner + j, b * inner + j) for a, b in pairs for j in range(inner)]
        return lax.ppermute(array, "ad", moves)

    def exchange(array):
        return lax.all_to_all(
            array, ("rep", "ad"), split_axis=0, concat_axis=0, tiled=True, axis_index_groups=planes
        )

    def adapt(rows, panel, model_width):
        latent = jnp.einsum(
            "sajd,ard->sajr", rows, panel[:, :, :model_width], preferred_element_type=F32
        ).astype(BF16)
        return (
            0.5 * jnp.einsum("sajr,arn->sajn", latent, panel[:, :, model_width:], preferred_element_type=F32)
        ).astype(BF16)

    def after(array, earlier):
        return lax.optimization_barrier((array, earlier))[0]

    def on_device(tokens, value_weight, down_weight, up_weight, request_adapter, adapter_home_slot):
        rows, model_width = tokens.shape
        resident = down_weight.shape[0]
        share = resident // reps
        adapters = adapter_home_slot.shape[0]
        rep = lax.axis_index("rep")
        here = lax.axis_index("ad") // inner
        own = jnp.concatenate(
            [
                lax.dynamic_slice_in_dim(down_weight, rep * share, share, 0).transpose(0, 2, 1),
                lax.dynamic_slice_in_dim(up_weight, rep * share, share, 0),
            ],
            axis=2,
        )
        labels = jnp.arange(adapters, dtype=jnp.int32)
        slot_of = jnp.sum(
            jnp.where(request_adapter[:, None] == labels[None, :], adapter_home_slot[None, :], 0),
            axis=1,
        )
        index = jnp.arange(rows, dtype=jnp.int32)
        earlier = (slot_of[:, None] == slot_of[None, :]) & (index[None, :] < index[:, None])
        position = jnp.sum(earlier.astype(jnp.int32), axis=1)
        owner, local = slot_of // resident, slot_of % resident
        layer, lane = owner // inner, owner % inner
        dest = (local // share) * inner + lane
        if relayed:
            low = here < 2
            middle = jnp.where(low, 2, 1)
            block = jnp.where(
                layer == here, 0, jnp.where(layer == here ^ 1, 1, jnp.where(layer == middle, 2, 3))
            )
        else:
            block = layer
        within = (local % share) * MOSTA + position
        span = share * MOSTA

        def places(start, count):
            at = jnp.arange(PLANE * count * span, dtype=jnp.int32)
            far = at // span
            return (far // count) * layers * span + (start + far % count) * span + at % span

        target = (dest * layers + block) * span + within

        def outgoing(start, count):
            pick = (places(start, count)[:, None] == target[None, :]).astype(BF16)
            sent = jnp.dot(pick, tokens, preferred_element_type=F32).astype(BF16)
            return sent.reshape(PLANE, count * share, MOSTA, model_width)

        def delta(update, start, count):
            pick = (target[:, None] == places(start, count)[None, :]).astype(BF16)
            return jnp.dot(pick, update.reshape(PLANE * count * span, -1), preferred_element_type=F32)

        def joined(parts):
            return jnp.concatenate(parts, axis=1)

        if relayed:
            edge = (here == 0) | (here == 3)
            far_rows = exchange(outgoing(3, 1))
            near_sent = outgoing(0, 3)
            near_rows = exchange(near_sent)
            pair = after(hop(own, (0, 1), (1, 0), (2, 3), (3, 2)), (far_rows, near_sent))
            mid = after(hop(own, (1, 2), (2, 1)), (far_rows, near_sent))
            crossed = hop(pair, (1, 2), (2, 1))
            outer = hop(mid, (1, 0), (2, 3))
            extra_rows = hop(far_rows, (0, 1), (3, 2))
            base = jnp.dot(tokens, lax.all_gather(value_weight, "ad", axis=0, tiled=True), preferred_element_type=F32)
            extra = hop(adapt(extra_rows, crossed, model_width), (1, 0), (2, 3))
            far = jnp.where(edge, extra, adapt(far_rows, crossed, model_width))
            panels = jnp.concatenate([own, pair, jnp.where(edge, outer, mid)], axis=0)
            near = adapt(near_rows, panels, model_width)
            back = exchange(joined([near, far]))
        else:
            sent = outgoing(0, layers)
            incoming = exchange(sent)
            panels = lax.all_gather(own, "ad", axis=0, tiled=True, axis_index_groups=columns)
            base = jnp.dot(tokens, lax.all_gather(value_weight, "ad", axis=0, tiled=True), preferred_element_type=F32)
            back = exchange(adapt(incoming, panels, model_width))
        return (base + delta(back, 0, layers)).astype(BF16)

    in_specs = (
        P(("rep", "ad"), None),
        P("ad", None),
        P("ad", None, None),
        P("ad", None, None),
        P(("rep", "ad")),
        P("rep"),
    )
    return jax.shard_map(
        on_device, mesh=mesh, in_specs=in_specs, out_specs=P(("rep", "ad"), None), check_vma=False
    )
```

```python
import jax
import jax.numpy as jnp
from jax import lax
from jax.sharding import PartitionSpec as P

MOSTA = 8
PLANE = 8
F32 = jnp.float32
BF16 = jnp.bfloat16


def solution(mesh):
    reps, devices = mesh.shape["rep"], mesh.shape["ad"]
    inner = PLANE // reps
    layers = devices // inner
    relayed = layers == 4
    columns = [[z * inner + j for z in range(layers)] for j in range(inner)]
    planes = [
        [r * devices + z * inner + j for r in range(reps) for j in range(inner)]
        for z in range(layers)
    ]

    def hop(array, *pairs):
        moves = [(a * inner + j, b * inner + j) for a, b in pairs for j in range(inner)]
        return lax.ppermute(array, "ad", moves)

    def exchange(array):
        return lax.all_to_all(
            array, ("rep", "ad"), split_axis=0, concat_axis=0, tiled=True, axis_index_groups=planes
        )

    def adapt(rows, panel, model_width):
        latent = jnp.einsum(
            "sajd,ard->sajr", rows, panel[:, :, :model_width], preferred_element_type=F32
        ).astype(BF16)
        return (
            0.5 * jnp.einsum("sajr,arn->sajn", latent, panel[:, :, model_width:], preferred_element_type=F32)
        ).astype(BF16)

    def after(array, earlier):
        return lax.optimization_barrier((array, earlier))[0]

    def on_device(tokens, value_weight, down_weight, up_weight, request_adapter, adapter_home_slot):
        rows, model_width = tokens.shape
        resident = down_weight.shape[0]
        share = resident // reps
        adapters = adapter_home_slot.shape[0]
        rep = lax.axis_index("rep")
        here = lax.axis_index("ad") // inner
        own = jnp.concatenate(
            [
                lax.dynamic_slice_in_dim(down_weight, rep * share, share, 0).transpose(0, 2, 1),
                lax.dynamic_slice_in_dim(up_weight, rep * share, share, 0),
            ],
            axis=2,
        )
        labels = jnp.arange(adapters, dtype=jnp.int32)
        slot_of = jnp.sum(
            jnp.where(request_adapter[:, None] == labels[None, :], adapter_home_slot[None, :], 0),
            axis=1,
        )
        index = jnp.arange(rows, dtype=jnp.int32)
        earlier = (slot_of[:, None] == slot_of[None, :]) & (index[None, :] < index[:, None])
        position = jnp.sum(earlier.astype(jnp.int32), axis=1)
        owner, local = slot_of // resident, slot_of % resident
        layer, lane = owner // inner, owner % inner
        dest = (local // share) * inner + lane
        if relayed:
            low = here < 2
            middle = jnp.where(low, 2, 1)
            block = jnp.where(
                layer == here, 0, jnp.where(layer == here ^ 1, 1, jnp.where(layer == middle, 2, 3))
            )
        else:
            block = layer
        within = (local % share) * MOSTA + position
        span = share * MOSTA

        def places(start, count):
            at = jnp.arange(PLANE * count * span, dtype=jnp.int32)
            far = at // span
            return (far // count) * layers * span + (start + far % count) * span + at % span

        target = (dest * layers + block) * span + within

        def outgoing(start, count):
            pick = (places(start, count)[:, None] == target[None, :]).astype(BF16)
            sent = jnp.dot(pick, tokens, preferred_element_type=F32).astype(BF16)
            return sent.reshape(PLANE, count * share, MOSTA, model_width)

        def delta(update, start, count):
            pick = (target[:, None] == places(start, count)[None, :]).astype(BF16)
            return jnp.dot(pick, update.reshape(PLANE * count * span, -1), preferred_element_type=F32)

        def joined(parts):
            return jnp.concatenate(parts, axis=1)

        if relayed:
            edge = (here == 0) | (here == 3)
            near_sent = outgoing(0, 3)
            far_rows = after(exchange(outgoing(3, 1)), near_sent)
            near_rows = exchange(near_sent)
            extra_rows = hop(far_rows, (0, 1), (3, 2))
            pair = after(hop(own, (0, 1), (1, 0), (2, 3), (3, 2)), extra_rows)
            mid = after(hop(own, (1, 2), (2, 1)), extra_rows)
            crossed = hop(pair, (1, 2), (2, 1))
            outer = hop(mid, (1, 0), (2, 3))
            base = jnp.dot(tokens, lax.all_gather(value_weight, "ad", axis=0, tiled=True), preferred_element_type=F32)
            extra = hop(adapt(extra_rows, crossed, model_width), (1, 0), (2, 3))
            far = jnp.where(edge, extra, adapt(far_rows, crossed, model_width))
            panels = jnp.concatenate([own, pair, jnp.where(edge, outer, mid)], axis=0)
            near = adapt(near_rows, panels, model_width)
            back = exchange(joined([near, far]))
        else:
            sent = outgoing(0, layers)
            incoming = exchange(sent)
            panels = lax.all_gather(own, "ad", axis=0, tiled=True, axis_index_groups=columns)
            base = jnp.dot(tokens, lax.all_gather(value_weight, "ad", axis=0, tiled=True), preferred_element_type=F32)
            back = exchange(adapt(incoming, panels, model_width))
        return (base + delta(back, 0, layers)).astype(BF16)

    in_specs = (
        P(("rep", "ad"), None),
        P("ad", None),
        P("ad", None, None),
        P("ad", None, None),
        P(("rep", "ad")),
        P("rep"),
    )
    return jax.shard_map(
        on_device, mesh=mesh, in_specs=in_specs, out_specs=P(("rep", "ad"), None), check_vma=False
    )
```

```python
import jax
import jax.numpy as jnp
from jax import lax
from jax.sharding import PartitionSpec as P

MOSTA = 8
PLANE = 8
F32 = jnp.float32
BF16 = jnp.bfloat16


def solution(mesh):
    reps, devices = mesh.shape["rep"], mesh.shape["ad"]
    inner = PLANE // reps
    layers = devices // inner
    relayed = layers == 4
    columns = [[z * inner + j for z in range(layers)] for j in range(inner)]
    planes = [
        [r * devices + z * inner + j for r in range(reps) for j in range(inner)]
        for z in range(layers)
    ]

    def hop(array, *pairs):
        moves = [(a * inner + j, b * inner + j) for a, b in pairs for j in range(inner)]
        return lax.ppermute(array, "ad", moves)

    def exchange(array):
        return lax.all_to_all(
            array, ("rep", "ad"), split_axis=0, concat_axis=0, tiled=True, axis_index_groups=planes
        )

    def adapt(rows, panel, model_width):
        latent = jnp.einsum(
            "sajd,ard->sajr", rows, panel[:, :, :model_width], preferred_element_type=F32
        ).astype(BF16)
        return (
            0.5 * jnp.einsum("sajr,arn->sajn", latent, panel[:, :, model_width:], preferred_element_type=F32)
        ).astype(BF16)

    def after(array, earlier):
        return lax.optimization_barrier((array, earlier))[0]

    def on_device(tokens, value_weight, down_weight, up_weight, request_adapter, adapter_home_slot):
        rows, model_width = tokens.shape
        resident = down_weight.shape[0]
        share = resident // reps
        adapters = adapter_home_slot.shape[0]
        rep = lax.axis_index("rep")
        here = lax.axis_index("ad") // inner
        own = jnp.concatenate(
            [
                lax.dynamic_slice_in_dim(down_weight, rep * share, share, 0).transpose(0, 2, 1),
                lax.dynamic_slice_in_dim(up_weight, rep * share, share, 0),
            ],
            axis=2,
        )
        labels = jnp.arange(adapters, dtype=jnp.int32)
        slot_of = jnp.sum(
            jnp.where(request_adapter[:, None] == labels[None, :], adapter_home_slot[None, :], 0),
            axis=1,
        )
        index = jnp.arange(rows, dtype=jnp.int32)
        earlier = (slot_of[:, None] == slot_of[None, :]) & (index[None, :] < index[:, None])
        position = jnp.sum(earlier.astype(jnp.int32), axis=1)
        owner, local = slot_of // resident, slot_of % resident
        layer, lane = owner // inner, owner % inner
        dest = (local // share) * inner + lane
        if relayed:
            low = here < 2
            middle = jnp.where(low, 2, 1)
            block = jnp.where(
                layer == here, 0, jnp.where(layer == here ^ 1, 1, jnp.where(layer == middle, 2, 3))
            )
        else:
            block = layer
        within = (local % share) * MOSTA + position
        span = share * MOSTA

        def places(start, count):
            at = jnp.arange(PLANE * count * span, dtype=jnp.int32)
            far = at // span
            return (far // count) * layers * span + (start + far % count) * span + at % span

        target = (dest * layers + block) * span + within

        def outgoing(start, count):
            pick = (places(start, count)[:, None] == target[None, :]).astype(BF16)
            sent = jnp.dot(pick, tokens, preferred_element_type=F32).astype(BF16)
            return sent.reshape(PLANE, count * share, MOSTA, model_width)

        def delta(update, start, count):
            pick = (target[:, None] == places(start, count)[None, :]).astype(BF16)
            return jnp.dot(pick, update.reshape(PLANE * count * span, -1), preferred_element_type=F32)

        def joined(parts):
            return jnp.concatenate(parts, axis=1)

        if relayed:
            edge = (here == 0) | (here == 3)
            far_rows = exchange(outgoing(3, 1))
            near_sent = outgoing(0, 3)
            near_rows = exchange(near_sent)
            pair = after(hop(own, (0, 1), (1, 0), (2, 3), (3, 2)), (far_rows, near_sent))
            mid = after(hop(own, (1, 2), (2, 1)), (far_rows, near_sent))
            crossed = hop(pair, (1, 2), (2, 1))
            outer = hop(mid, (1, 0), (2, 3))
            extra_rows = hop(far_rows, (0, 1), (3, 2))
            base = jnp.dot(tokens, lax.all_gather(value_weight, "ad", axis=0, tiled=True), preferred_element_type=F32)
            extra = hop(adapt(extra_rows, crossed, model_width), (1, 0), (2, 3))
            panels = jnp.concatenate([own, pair, jnp.where(edge, outer, mid)], axis=0)
            near = adapt(near_rows, panels, model_width)
            local = adapt(far_rows, crossed, model_width)
            far = jnp.where(edge, after(extra, (near, local)), local)
            back = exchange(joined([near, far]))
        else:
            sent = outgoing(0, layers)
            incoming = exchange(sent)
            panels = lax.all_gather(own, "ad", axis=0, tiled=True, axis_index_groups=columns)
            base = jnp.dot(tokens, lax.all_gather(value_weight, "ad", axis=0, tiled=True), preferred_element_type=F32)
            back = exchange(adapt(incoming, panels, model_width))
        return (base + delta(after(back, base), 0, layers)).astype(BF16)

    in_specs = (
        P(("rep", "ad"), None),
        P("ad", None),
        P("ad", None, None),
        P("ad", None, None),
        P(("rep", "ad")),
        P("rep"),
    )
    return jax.shard_map(
        on_device, mesh=mesh, in_specs=in_specs, out_specs=P(("rep", "ad"), None), check_vma=False
    )
```

```python
import jax
import jax.numpy as jnp
from jax import lax
from jax.sharding import PartitionSpec as P

MOSTA = 8
PLANE = 8
F32 = jnp.float32
BF16 = jnp.bfloat16


def solution(mesh):
    reps, devices = mesh.shape["rep"], mesh.shape["ad"]
    inner = PLANE // reps
    layers = devices // inner
    relayed = layers == 4
    columns = [[z * inner + j for z in range(layers)] for j in range(inner)]
    planes = [
        [r * devices + z * inner + j for r in range(reps) for j in range(inner)]
        for z in range(layers)
    ]

    def hop(array, *pairs):
        moves = [(a * inner + j, b * inner + j) for a, b in pairs for j in range(inner)]
        return lax.ppermute(array, "ad", moves)

    def exchange(array):
        return lax.all_to_all(
            array, ("rep", "ad"), split_axis=0, concat_axis=0, tiled=True, axis_index_groups=planes
        )

    def adapt(rows, panel, model_width):
        latent = jnp.einsum(
            "sajd,ard->sajr", rows, panel[:, :, :model_width], preferred_element_type=F32
        ).astype(BF16)
        return (
            0.5 * jnp.einsum("sajr,arn->sajn", latent, panel[:, :, model_width:], preferred_element_type=F32)
        ).astype(BF16)

    def after(array, earlier):
        return lax.optimization_barrier((array, earlier))[0]

    def on_device(tokens, value_weight, down_weight, up_weight, request_adapter, adapter_home_slot):
        rows, model_width = tokens.shape
        resident = down_weight.shape[0]
        share = resident // reps
        adapters = adapter_home_slot.shape[0]
        rep = lax.axis_index("rep")
        here = lax.axis_index("ad") // inner
        own = jnp.concatenate(
            [
                lax.dynamic_slice_in_dim(down_weight, rep * share, share, 0).transpose(0, 2, 1),
                lax.dynamic_slice_in_dim(up_weight, rep * share, share, 0),
            ],
            axis=2,
        )
        labels = jnp.arange(adapters, dtype=jnp.int32)
        slot_of = jnp.sum(
            jnp.where(request_adapter[:, None] == labels[None, :], adapter_home_slot[None, :], 0),
            axis=1,
        )
        index = jnp.arange(rows, dtype=jnp.int32)
        earlier = (slot_of[:, None] == slot_of[None, :]) & (index[None, :] < index[:, None])
        position = jnp.sum(earlier.astype(jnp.int32), axis=1)
        owner, local = slot_of // resident, slot_of % resident
        layer, lane = owner // inner, owner % inner
        dest = (local // share) * inner + lane
        if relayed:
            low = here < 2
            middle = jnp.where(low, 2, 1)
            block = jnp.where(
                layer == here, 0, jnp.where(layer == here ^ 1, 1, jnp.where(layer == middle, 2, 3))
            )
        else:
            block = layer
        within = (local % share) * MOSTA + position
        span = share * MOSTA

        def places(start, count):
            at = jnp.arange(PLANE * count * span, dtype=jnp.int32)
            far = at // span
            return (far // count) * layers * span + (start + far % count) * span + at % span

        target = (dest * layers + block) * span + within

        def outgoing(start, count):
            pick = (places(start, count)[:, None] == target[None, :]).astype(BF16)
            sent = jnp.dot(pick, tokens, preferred_element_type=F32).astype(BF16)
            return sent.reshape(PLANE, count * share, MOSTA, model_width)

        def delta(update, start, count):
            pick = (target[:, None] == places(start, count)[None, :]).astype(BF16)
            return jnp.dot(pick, update.reshape(PLANE * count * span, -1), preferred_element_type=F32)

        def joined(parts):
            return jnp.concatenate(parts, axis=1)

        if relayed:
            edge = (here == 0) | (here == 3)
            far_rows = exchange(outgoing(3, 1))
            near_sent = outgoing(0, 3)
            near_rows = exchange(near_sent)
            pair = after(hop(own, (0, 1), (1, 0), (2, 3), (3, 2)), (far_rows, near_sent))
            mid = after(hop(own, (1, 2), (2, 1)), (far_rows, near_sent))
            crossed = hop(pair, (1, 2), (2, 1))
            outer = hop(mid, (1, 0), (2, 3))
            extra_rows = hop(far_rows, (0, 1), (3, 2))
            base = jnp.dot(tokens, lax.all_gather(value_weight, "ad", axis=0, tiled=True), preferred_element_type=F32)
            extra = hop(adapt(extra_rows, crossed, model_width), (1, 0), (2, 3))
            far = jnp.where(edge, extra, adapt(far_rows, crossed, model_width))
            panels = jnp.concatenate([own, pair, jnp.where(edge, outer, mid)], axis=0)
            near = adapt(near_rows, panels, model_width)
            back = exchange(joined([near, far]))
        else:
            sent = outgoing(0, layers)
            incoming = exchange(sent)
            panels = lax.all_gather(own, "ad", axis=0, tiled=True, axis_index_groups=columns)
            base = jnp.dot(tokens, lax.all_gather(value_weight, "ad", axis=0, tiled=True), preferred_element_type=F32)
            back = exchange(adapt(incoming, panels, model_width))
        return (base + delta(after(back, base), 0, layers)).astype(BF16)

    in_specs = (
        P(("rep", "ad"), None),
        P("ad", None),
        P("ad", None, None),
        P("ad", None, None),
        P(("rep", "ad")),
        P("rep"),
    )
    return jax.shard_map(
        on_device, mesh=mesh, in_specs=in_specs, out_specs=P(("rep", "ad"), None), check_vma=False
    )
```
